32 devices in a mesh: red: 4 (over y, x), rep: 8 (over z, core).
Axes of the slice: x: 2, y: 2, z: 4, core: 2. Of those that a mesh axis runs over, the one named last changes fastest.
Arguments:
- amplitudes: float32 [8, 32, 8192], P(None, 'rep', 'red'), may hold values from -6 to 6
- integrals: float32 [8, 2048, 8192], P(None, 'red', 'rep'), may hold values from -0.0625 to 0.0625
Outputs:
- ladder: float32 [8, 32, 2048], P(None, 'rep', 'red')
The draws below stay inside these ranges and needn't reach their ends.
All inputs are finite; a program needn't handle non-finite values.
Results may differ from the reference program's by a relative error of at most 0.00007.
Values sent between devices are 32-bit elements; how exact they have to be, the bound alone decides.
A program may use at most 64 MiB of HBM per device.

```python
import jax
import jax.numpy as jnp
from jax import lax

NIRREP = 8
CD = 8192
AB = 2048
IJ = 32


def levels(own_key, shape, shards, smallest, high):
    def one(position, parts):
        draws = jax.random.uniform(jax.random.fold_in(jax.random.fold_in(own_key, 6), position), (parts,), jnp.float32, smallest / len(shards), high / len(shards))
        return jnp.repeat(jnp.exp(draws), shape[position] // parts).reshape((-1,) + (1,) * (len(shape) - position - 1))

    gain = one(*shards[0])
    for cut in shards[1:]:
        gain = gain * one(*cut)
    return gain


def scatter_about(stream_key, extent, spread, most, cuts=(), held_as=jnp.bfloat16):
    level = levels(stream_key, extent, cuts, -0.22, 0.18) if cuts else 1.0
    array = jax.random.normal(stream_key, extent, jnp.float32) * spread * level
    return jnp.minimum(jnp.maximum(array, -most), most).astype(held_as)


def setup_inputs(seed: int = 0) -> dict:
    arg_keys = jax.random.split(jax.random.key(seed), 3)
    amplitudes = scatter_about(arg_keys[0], (NIRREP, IJ, CD), 1.0, 6.0, ((1, 8), (2, 4)), jnp.float32)
    integrals = scatter_about(arg_keys[1], (NIRREP, AB, CD), CD ** -0.5, 0.0625, ((1, 4), (2, 8)), jnp.float32)
    return {"amplitudes": amplitudes, "integrals": integrals}


def reference(amplitudes, integrals):
    contracted = jnp.einsum("gic,gac->gia", amplitudes, integrals, precision=lax.Precision.HIGHEST)
    return 0.5 * contracted
```

```python
import functools

import jax
import jax.numpy as jnp
from jax import lax
from jax.experimental import pallas as pl
from jax.experimental.pallas import tpu as pltpu
from jax.sharding import PartitionSpec as P

MESH = pl.DeviceIdType.MESH


def contract(rows_block, integrals):
    return jnp.einsum("gic,gac->gia", rows_block, integrals, precision=lax.Precision.HIGHEST)


def per_device_collectives(amplitudes, integrals):
    full_pairs = lax.all_gather(amplitudes, "red", axis=2, tiled=True)
    ordered = lax.all_to_all(full_pairs, "rep", split_axis=2, concat_axis=1, tiled=True)
    partial_value = contract(ordered, integrals)
    contracted = lax.psum_scatter(partial_value, "rep", scatter_dimension=1, tiled=True)
    return 0.5 * contracted


def ladder_kernel(
    amp, integ, out,
    raw, high, low, buf, part, from_core, summed, from_z,
    raw_sem, scatter_send, scatter_recv, plane_send, plane_recv, diag_send, diag_recv,
    core_send, core_recv, z_send, z_recv,
):
    n_rep, rows, cols = buf.shape[1:]
    half = n_rep // 2
    r, p = lax.axis_index("red"), lax.axis_index("rep")
    z, c = p // 2, p % 2
    x, y = r % 2, r // 2
    x_nbr = (1 - x) + 2 * y
    y_nbr = x + 2 * (1 - y)
    diag = (1 - x) + 2 * (1 - y)
    order = [(r, 0), (r, 1), (x_nbr, 0), (y_nbr, 0), (x_nbr, 1), (y_nbr, 1), (diag, 0), (diag, 1)]
    sym = [2 * q + j for q, j in order]

    def load(t):
        return pltpu.make_async_copy(integ.at[sym[t]], raw.at[t], raw_sem.at[t])

    for t in range(8):
        load(t).start()

    barrier = pltpu.get_barrier_semaphore()
    on_own = z == r

    def greet(red, rep):
        pl.semaphore_signal(barrier, inc=1, device_id=(red, rep), device_id_type=MESH)

    for k in range(1, n_rep):
        greet(z, (p + k) % n_rep)

    @pl.when(jnp.logical_not(on_own))
    def _():
        greet(z, p)

    greet(x_nbr, p)
    greet(y_nbr, p)
    greet(r, 2 * z + (1 - c))
    for k in range(1, 4):
        greet(r, 2 * ((z + k) % 4) + c)

    @pl.when(on_own)
    def _():
        pl.semaphore_wait(barrier, 13)

    @pl.when(jnp.logical_not(on_own))
    def _():
        pl.semaphore_wait(barrier, 14)

    def scatter(j, k, h):
        q = (r + k) % 4
        g = 2 * q + j
        src = amp.at[g, :, pl.ds(h * cols, cols)]
        dst = buf.at[g, p]
        target = 2 * r + h
        remote = pltpu.make_async_remote_copy(
            src_ref=src, dst_ref=dst, send_sem=scatter_send.at[j, k, h], recv_sem=scatter_recv.at[j],
            device_id=(q, target), device_id_type=MESH,
        )
        local = pltpu.make_async_copy(src, dst, scatter_recv.at[j])
        mine = jnp.logical_and(on_own, c == h) if k == 0 else None
        return remote, local, mine

    def scatter_all(act):
        for j in range(2):
            for k in range(4):
                for h in range(2):
                    remote, local, mine = scatter(j, k, h)
                    if mine is None:
                        act(remote)
                    else:
                        pl.when(jnp.logical_not(mine))(functools.partial(act, remote))
                        if act is start:
                            pl.when(mine)(local.start)

    def start(copy):
        copy.start()

    def wait_send(copy):
        copy.wait_send()

    scatter_all(start)

    def plane(j, way):
        g = 2 * r + j
        return pltpu.make_async_remote_copy(
            src_ref=buf.at[g], dst_ref=buf.at[g], send_sem=plane_send.at[j, way], recv_sem=plane_recv.at[j, way],
            device_id=((x_nbr, y_nbr)[way], p), device_id_type=MESH,
        )

    def onward(j, way):
        g = 2 * (x_nbr, y_nbr)[way] + j
        piece = buf.at[g, pl.ds(way * half, half)]
        return pltpu.make_async_remote_copy(
            src_ref=piece, dst_ref=piece, send_sem=diag_send.at[j, way], recv_sem=diag_recv.at[j],
            device_id=((y_nbr, x_nbr)[way], p), device_id_type=MESH,
        )

    def arrived(sem, ref):
        pltpu.make_async_copy(ref, ref, sem).wait()

    def own(j):
        arrived(scatter_recv.at[j], buf.at[2 * r + j])
        plane(j, 0).start()
        plane(j, 1).start()

    def from_plane(j, way):
        arrived(plane_recv.at[j, way], buf.at[2 * (x_nbr, y_nbr)[way] + j])
        onward(j, way).start()

    def from_diag(j):
        arrived(diag_recv.at[j], buf.at[2 * diag + j])

    step = 64
    n_a = raw.shape[1]

    def split(t):
        load(t).wait()

        @pl.loop(0, n_a // step)
        def _(s):
            here = pl.ds(pl.multiple_of(s * step, step), step)
            value = raw[t, here, :]
            top = value.astype(jnp.bfloat16)
            high[t, here, :] = top
            low[t, here, :] = (value - top.astype(jnp.float32)).astype(jnp.bfloat16)

    dims = (((1,), (1,)), ((), ()))
    n_i = n_rep * rows

    def to_core(t):
        return pltpu.make_async_remote_copy(
            src_ref=part.at[t, 1 - c], dst_ref=from_core.at[t], send_sem=core_send.at[t], recv_sem=core_recv.at[t],
            device_id=(r, 2 * z + (1 - c)), device_id_type=MESH,
        )

    def multiply(t):
        g = sym[t]
        value = jnp.concatenate([buf[g, k] for k in range(n_rep)], axis=0)
        top = value.astype(jnp.bfloat16)
        rest = (value - top.astype(jnp.float32)).astype(jnp.bfloat16)
        both = lax.dot_general(
            jnp.concatenate([top, rest], axis=0), high[t], dims, preferred_element_type=jnp.float32
        )
        more = lax.dot_general(top, low[t], dims, preferred_element_type=jnp.float32)
        product = both[:n_i] + (both[n_i:] + more)
        for k in range(n_rep):
            part[t, k % 2, k // 2] = product[k * rows:(k + 1) * rows]
        to_core(t).start()

    def to_z(t, k):
        there = (z + k) % 4
        return pltpu.make_async_remote_copy(
            src_ref=summed.at[t, there], dst_ref=from_z.at[t, k - 1], send_sem=z_send.at[t, k - 1],
            recv_sem=z_recv.at[t], device_id=(r, 2 * there + c), device_id_type=MESH,
        )

    def send_z(t):
        to_core(t).wait_recv()
        summed[t] = part[t, c] + from_core[t]
        for k in range(1, 4):
            to_z(t, k).start()

    def finish(t):
        arrived(z_recv.at[t], from_z.at[t])
        total = (summed[t, z] + from_z[t, 0]) + (from_z[t, 1] + from_z[t, 2])
        out[sym[t]] = 0.5 * total

    split(0)
    split(1)
    own(0)
    split(2)
    split(3)
    own(1)
    multiply(0)
    multiply(1)
    split(4)
    from_plane(0, 0)
    from_plane(0, 1)
    send_z(0)
    send_z(1)
    multiply(2)
    multiply(3)
    split(5)
    from_plane(1, 0)
    from_plane(1, 1)
    send_z(2)
    send_z(3)
    multiply(4)
    multiply(5)
    split(6)
    split(7)
    send_z(4)
    send_z(5)
    from_diag(0)
    multiply(6)
    from_diag(1)
    multiply(7)
    send_z(6)
    for t in range(4):
        finish(t)
    send_z(7)
    for t in range(4, 8):
        finish(t)

    scatter_all(wait_send)
    for j in range(2):
        for way in range(2):
            plane(j, way).wait_send()
            onward(j, way).wait_send()
    for t in range(8):
        to_core(t).wait_send()
        for k in range(1, 4):
            to_z(t, k).wait_send()


def per_device_kernel(amplitudes, integrals):
    n_sym, rows, _ = amplitudes.shape
    _, n_a, cols = integrals.shape
    n_rep = 8
    f32, bf16 = jnp.float32, jnp.bfloat16
    dma = pltpu.SemaphoreType.DMA
    return pl.pallas_call(
        ladder_kernel,
        out_shape=jax.ShapeDtypeStruct((n_sym, rows, n_a), f32),
        in_specs=[pl.BlockSpec(memory_space=pl.ANY)] * 2,
        out_specs=pl.BlockSpec(memory_space=pltpu.VMEM),
        scratch_shapes=[
            pltpu.VMEM((n_sym, n_a, cols), f32),
            pltpu.VMEM((n_sym, n_a, cols), bf16),
            pltpu.VMEM((n_sym, n_a, cols), bf16),
            pltpu.VMEM((n_sym, n_rep, rows, cols), f32),
            pltpu.VMEM((n_sym, 2, n_rep // 2, rows, n_a), f32),
            pltpu.VMEM((n_sym, n_rep // 2, rows, n_a), f32),
            pltpu.VMEM((n_sym, n_rep // 2, rows, n_a), f32),
            pltpu.VMEM((n_sym, n_rep // 2 - 1, rows, n_a), f32),
            dma((8,)),
            dma((2, 4, 2)),
            dma((2,)),
            dma((2, 2)),
            dma((2, 2)),
            dma((2, 2)),
            dma((2,)),
            dma((8,)),
            dma((8,)),
            dma((8, 3)),
            dma((8,)),
        ],
        compiler_params=pltpu.CompilerParams(
            collective_id=0, has_side_effects=True, vmem_limit_bytes=48 * 2**20
        ),
        cost_estimate=pl.CostEstimate(
            flops=6 * n_sym * n_rep * rows * n_a * cols, bytes_accessed=integrals.size * 4, transcendentals=0
        ),
    )(amplitudes, integrals)


def solution(mesh):
    in_specs = (P(None, "rep", "red"), P(None, "red", "rep"))
    out_specs = P(None, "rep", "red")
    fits = mesh.shape["red"] == 4 and mesh.shape["rep"] == 8
    return jax.shard_map(
        per_device_kernel if fits else per_device_collectives,
        mesh=mesh, in_specs=in_specs, out_specs=out_specs, check_vma=False,
    )
```

```python
import functools

import jax
import jax.numpy as jnp
from jax import lax
from jax.experimental import pallas as pl
from jax.experimental.pallas import tpu as pltpu
from jax.sharding import PartitionSpec as P

MESH = pl.DeviceIdType.MESH


def contract(rows_block, integrals):
    return jnp.einsum("gic,gac->gia", rows_block, integrals, precision=lax.Precision.HIGHEST)


def per_device_collectives(amplitudes, integrals):
    full_pairs = lax.all_gather(amplitudes, "red", axis=2, tiled=True)
    ordered = lax.all_to_all(full_pairs, "rep", split_axis=2, concat_axis=1, tiled=True)
    partial_value = contract(ordered, integrals)
    contracted = lax.psum_scatter(partial_value, "rep", scatter_dimension=1, tiled=True)
    return 0.5 * contracted


def ladder_kernel(
    amp, integ, out,
    raw, high, low, stage, buf, part, from_core, summed, from_z,
    raw_sem, spread_send, spread_recv, column_send, column_recv, plane_send, plane_recv, diag_send, diag_recv,
    core_send, core_recv, z_send, z_recv,
):
    n_rep, rows, cols = buf.shape[1:]
    half = n_rep // 2
    r, p = lax.axis_index("red"), lax.axis_index("rep")
    z, c = p // 2, p % 2
    x, y = r % 2, r // 2
    x_nbr = (1 - x) + 2 * y
    y_nbr = x + 2 * (1 - y)
    diag = (1 - x) + 2 * (1 - y)
    order = [(r, 0), (r, 1), (x_nbr, 0), (y_nbr, 0), (x_nbr, 1), (y_nbr, 1), (diag, 0), (diag, 1)]
    sym = [2 * q + j for q, j in order]

    def load(t):
        return pltpu.make_async_copy(integ.at[sym[t]], raw.at[t], raw_sem.at[t])

    for t in range(8):
        load(t).start()

    barrier = pltpu.get_barrier_semaphore()
    peers = [(x_nbr, p), (y_nbr, p), (diag, p)] + [(r, (p + k) % n_rep) for k in range(1, n_rep)]
    for peer in peers:
        pl.semaphore_signal(barrier, inc=1, device_id=peer, device_id_type=MESH)
    pl.semaphore_wait(barrier, len(peers))

    near = [r, x_nbr, y_nbr, diag]

    def spread(j, k):
        return pltpu.make_async_remote_copy(
            src_ref=amp.at[2 * near[k] + j], dst_ref=stage.at[j, k - 1], send_sem=spread_send.at[j, k - 1],
            recv_sem=spread_recv.at[j, k - 1], device_id=(near[k], p), device_id_type=MESH,
        )

    def column(j, k, h, act):
        here = pl.ds(h * cols, cols)
        src = amp.at[2 * r + j, :, here] if k == 0 else stage.at[j, k - 1, :, here]
        dst = buf.at[2 * r + j, p]
        target = 2 * near[k] + h
        mine = target == p

        @pl.when(jnp.logical_not(mine))
        def _():
            act(pltpu.make_async_remote_copy(
                src_ref=src, dst_ref=dst, send_sem=column_send.at[j, k, h], recv_sem=column_recv.at[j, z],
                device_id=(r, target), device_id_type=MESH,
            ))

        if act is start:
            @pl.when(mine)
            def _():
                pltpu.make_async_copy(src, dst, column_recv.at[j, z]).start()

    def start(copy):
        copy.start()

    def wait_send(copy):
        copy.wait_send()

    def column_all(j, k, act):
        for h in range(2):
            column(j, k, h, act)

    for j in range(2):
        for k in range(1, 4):
            spread(j, k).start()
    for j in range(2):
        column_all(j, 0, start)

    upper = z // 2
    z_order = [z, 2 * upper + 1 - z % 2, 2 - upper, 3 - 3 * upper]

    def plane(j, n, way):
        piece = buf.at[2 * r + j, pl.ds(2 * z_order[n], 2)]
        return pltpu.make_async_remote_copy(
            src_ref=piece, dst_ref=piece, send_sem=plane_send.at[j, n, way], recv_sem=plane_recv.at[j, way, n // 2],
            device_id=((x_nbr, y_nbr)[way], p), device_id_type=MESH,
        )

    def half_of(g, n):
        first = upper if n == 0 else 1 - upper
        return buf.at[g, pl.ds(first * half, half)]

    def onward(j, way):
        piece = half_of(2 * (x_nbr, y_nbr)[way] + j, way)
        return pltpu.make_async_remote_copy(
            src_ref=piece, dst_ref=piece, send_sem=diag_send.at[j, way], recv_sem=diag_recv.at[j],
            device_id=((y_nbr, x_nbr)[way], p), device_id_type=MESH,
        )

    def arrived(sem, ref):
        pltpu.make_async_copy(ref, ref, sem).wait()

    def relay(j):
        for k in range(1, 4):
            arrived(spread_recv.at[j, k - 1], stage.at[j, k - 1])
            column_all(j, k, start)

    def own(j):
        for n in range(4):
            arrived(column_recv.at[j, z_order[n]], buf.at[2 * r + j, pl.ds(2 * z_order[n], 2)])
            plane(j, n, 0).start()
            plane(j, n, 1).start()

    def from_plane(j):
        for n in range(2):
            for way in range(2):
                arrived(plane_recv.at[j, way, n], half_of(2 * (x_nbr, y_nbr)[way] + j, n))
                if n == way:
                    onward(j, way).start()

    def from_diag(j):
        arrived(diag_recv.at[j], buf.at[2 * diag + j])

    step = 64
    n_a = raw.shape[1]

    def split(t):
        load(t).wait()

        @pl.loop(0, n_a // step)
        def _(s):
            here = pl.ds(pl.multiple_of(s * step, step), step)
            value = raw[t, here, :]
            top = value.astype(jnp.bfloat16)
            high[t, here, :] = top
            low[t, here, :] = (value - top.astype(jnp.float32)).astype(jnp.bfloat16)

    dims = (((1,), (1,)), ((), ()))
    n_i = n_rep * rows

    def to_core(t):
        return pltpu.make_async_remote_copy(
            src_ref=part.at[t, 1 - c], dst_ref=from_core.at[t], send_sem=core_send.at[t], recv_sem=core_recv.at[t],
            device_id=(r, 2 * z + (1 - c)), device_id_type=MESH,
        )

    def multiply(t):
        g = sym[t]
        value = jnp.concatenate([buf[g, k] for k in range(n_rep)], axis=0)
        top = value.astype(jnp.bfloat16)
        rest = (value - top.astype(jnp.float32)).astype(jnp.bfloat16)
        both = lax.dot_general(
            jnp.concatenate([top, rest], axis=0), high[t], dims, preferred_element_type=jnp.float32
        )
        more = lax.dot_general(top, low[t], dims, preferred_element_type=jnp.float32)
        product = both[:n_i] + (both[n_i:] + more)
        for k in range(n_rep):
            part[t, k % 2, k // 2] = product[k * rows:(k + 1) * rows]
        to_core(t).start()

    def to_z(t, k):
        there = (z + k) % 4
        return pltpu.make_async_remote_copy(
            src_ref=summed.at[t, there], dst_ref=from_z.at[t, k - 1], send_sem=z_send.at[t, k - 1],
            recv_sem=z_recv.at[t], device_id=(r, 2 * there + c), device_id_type=MESH,
        )

    def send_z(t):
        to_core(t).wait_recv()
        summed[t] = part[t, c] + from_core[t]
        for k in range(1, 4):
            to_z(t, k).start()

    def finish(t):
        arrived(z_recv.at[t], from_z.at[t])
        total = (summed[t, z] + from_z[t, 0]) + (from_z[t, 1] + from_z[t, 2])
        out[sym[t]] = 0.5 * total

    relay(0)
    relay(1)
    split(0)
    split(1)
    own(0)
    split(2)
    split(3)
    own(1)
    multiply(0)
    multiply(1)
    split(4)
    from_plane(0)
    send_z(0)
    send_z(1)
    multiply(2)
    multiply(3)
    split(5)
    from_plane(1)
    send_z(2)
    send_z(3)
    multiply(4)
    multiply(5)
    split(6)
    split(7)
    send_z(4)
    send_z(5)
    from_diag(0)
    multiply(6)
    from_diag(1)
    multiply(7)
    send_z(6)
    for t in range(4):
        finish(t)
    send_z(7)
    for t in range(4, 8):
        finish(t)

    for j in range(2):
        for k in range(1, 4):
            spread(j, k).wait_send()
        for k in range(4):
            column_all(j, k, wait_send)
        for way in range(2):
            for n in range(4):
                plane(j, n, way).wait_send()
            onward(j, way).wait_send()
    for t in range(8):
        to_core(t).wait_send()
        for k in range(1, 4):
            to_z(t, k).wait_send()


def per_device_kernel(amplitudes, integrals):
    n_sym, rows, _ = amplitudes.shape
    _, n_a, cols = integrals.shape
    n_rep = 8
    f32, bf16 = jnp.float32, jnp.bfloat16
    dma = pltpu.SemaphoreType.DMA
    return pl.pallas_call(
        ladder_kernel,
        out_shape=jax.ShapeDtypeStruct((n_sym, rows, n_a), f32),
        in_specs=[pl.BlockSpec(memory_space=pl.ANY)] * 2,
        out_specs=pl.BlockSpec(memory_space=pltpu.VMEM),
        scratch_shapes=[
            pltpu.VMEM((n_sym, n_a, cols), f32),
            pltpu.VMEM((n_sym, n_a, cols), bf16),
            pltpu.VMEM((n_sym, n_a, cols), bf16),
            pltpu.VMEM((2, 3, rows, amplitudes.shape[2]), f32),
            pltpu.VMEM((n_sym, n_rep, rows, cols), f32),
            pltpu.VMEM((n_sym, 2, n_rep // 2, rows, n_a), f32),
            pltpu.VMEM((n_sym, n_rep // 2, rows, n_a), f32),
            pltpu.VMEM((n_sym, n_rep // 2, rows, n_a), f32),
            pltpu.VMEM((n_sym, n_rep // 2 - 1, rows, n_a), f32),
            dma((8,)),
            dma((2, 3)),
            dma((2, 3)),
            dma((2, 4, 2)),
            dma((2, 4)),
            dma((2, 4, 2)),
            dma((2, 2, 2)),
            dma((2, 2)),
            dma((2,)),
            dma((8,)),
            dma((8,)),
            dma((8, 3)),
            dma((8,)),
        ],
        compiler_params=pltpu.CompilerParams(
            collective_id=0, has_side_effects=True, vmem_limit_bytes=48 * 2**20
        ),
        cost_estimate=pl.CostEstimate(
            flops=6 * n_sym * n_rep * rows * n_a * cols, bytes_accessed=integrals.size * 4, transcendentals=0
        ),
    )(amplitudes, integrals)


def solution(mesh):
    in_specs = (P(None, "rep", "red"), P(None, "red", "rep"))
    out_specs = P(None, "rep", "red")
    fits = mesh.shape["red"] == 4 and mesh.shape["rep"] == 8
    return jax.shard_map(
        per_device_kernel if fits else per_device_collectives,
        mesh=mesh, in_specs=in_specs, out_specs=out_specs, check_vma=False,
    )
```

```python
import functools

import jax
import jax.numpy as jnp
from jax import lax
from jax.experimental import pallas as pl
from jax.experimental.pallas import tpu as pltpu
from jax.sharding import PartitionSpec as P

MESH = pl.DeviceIdType.MESH


def contract(rows_block, integrals):
    return jnp.einsum("gic,gac->gia", rows_block, integrals, precision=lax.Precision.HIGHEST)


def per_device_collectives(amplitudes, integrals):
    full_pairs = lax.all_gather(amplitudes, "red", axis=2, tiled=True)
    ordered = lax.all_to_all(full_pairs, "rep", split_axis=2, concat_axis=1, tiled=True)
    partial_value = contract(ordered, integrals)
    contracted = lax.psum_scatter(partial_value, "rep", scatter_dimension=1, tiled=True)
    return 0.5 * contracted


def ladder_kernel(
    amp, integ, out,
    raw, high, low, stage, buf, part, from_core, summed, from_z,
    raw_sem, spread_send, spread_recv, column_send, column_recv, plane_send, plane_recv, diag_send, diag_recv,
    core_send, core_recv, z_send, z_recv, known,
):
    n_rep, rows, cols = buf.shape[1:]
    half = n_rep // 2
    r, p = lax.axis_index("red"), lax.axis_index("rep")
    z, c = p // 2, p % 2
    x, y = r % 2, r // 2
    x_nbr = (1 - x) + 2 * y
    y_nbr = x + 2 * (1 - y)
    diag = (1 - x) + 2 * (1 - y)
    order = [(r, 0), (r, 1), (x_nbr, 0), (y_nbr, 0), (x_nbr, 1), (y_nbr, 1), (diag, 0), (diag, 1)]
    sym = [2 * q + j for q, j in order]

    def load(t):
        return pltpu.make_async_copy(integ.at[sym[t]], raw.at[t], raw_sem.at[t])

    for t in range(8):
        load(t).start()

    barrier = pltpu.get_barrier_semaphore()
    last = n_rep // 2 - 1
    has_below, has_above = z > 0, z < last

    def signal(sem, red, rep):
        pl.semaphore_signal(sem, inc=1, device_id=(red, rep), device_id_type=MESH)

    for red in (diag, x_nbr, y_nbr):
        signal(barrier, red, p)
    signal(barrier, r, 2 * z + (1 - c))

    @pl.when(has_below)
    def _():
        for h in range(2):
            signal(barrier, r, 2 * (z - 1) + h)

    @pl.when(has_above)
    def _():
        for h in range(2):
            signal(barrier, r, 2 * (z + 1) + h)

    inner = jnp.logical_and(has_below, has_above)


    @pl.when(inner)
    def _():
        pl.semaphore_wait(barrier, 8)

    @pl.when(jnp.logical_not(inner))
    def _():
        pl.semaphore_wait(barrier, 6)

    def tell(n):
        @pl.when(has_below)
        def _():
            signal(known.at[n], r, p - 2)

        @pl.when(has_above)
        def _():
            signal(known.at[n], r, p + 2)

    def hear(n):
        @pl.when(inner)
        def _():
            pl.semaphore_wait(known.at[n], 2)

        @pl.when(jnp.logical_not(inner))
        def _():
            pl.semaphore_wait(known.at[n], 1)

    near = [r, x_nbr, y_nbr, diag]

    def spread(j, k):
        return pltpu.make_async_remote_copy(
            src_ref=amp.at[2 * near[k] + j], dst_ref=stage.at[j, k - 1], send_sem=spread_send.at[j, k - 1],
            recv_sem=spread_recv.at[j, k - 1], device_id=(near[k], p), device_id_type=MESH,
        )

    def column(j, k, h, act):
        here = pl.ds(h * cols, cols)
        src = amp.at[2 * r + j, :, here] if k == 0 else stage.at[j, k - 1, :, here]
        dst = buf.at[2 * r + j, p]
        target = 2 * near[k] + h
        mine = target == p

        @pl.when(jnp.logical_not(mine))
        def _():
            act(pltpu.make_async_remote_copy(
                src_ref=src, dst_ref=dst, send_sem=column_send.at[j, k, h], recv_sem=column_recv.at[j, z],
                device_id=(r, target), device_id_type=MESH,
            ))

        if act is start:
            @pl.when(mine)
            def _():
                pltpu.make_async_copy(src, dst, column_recv.at[j, z]).start()

    def start(copy):
        copy.start()

    def wait_send(copy):
        copy.wait_send()

    def column_all(j, k, act):
        for h in range(2):
            column(j, k, h, act)

    for j in range(2):
        for k in range(1, 4):
            spread(j, k).start()
    tell(0)

    upper = z // 2
    z_order = [z, 2 * upper + 1 - z % 2, 2 - upper, 3 - 3 * upper]

    def plane(j, n, way):
        piece = buf.at[2 * r + j, pl.ds(2 * z_order[n], 2)]
        return pltpu.make_async_remote_copy(
            src_ref=piece, dst_ref=piece, send_sem=plane_send.at[j, n, way], recv_sem=plane_recv.at[j, way, n // 2],
            device_id=((x_nbr, y_nbr)[way], p), device_id_type=MESH,
        )

    def half_of(g, n):
        first = upper if n == 0 else 1 - upper
        return buf.at[g, pl.ds(first * half, half)]

    def onward(j, way):
        piece = half_of(2 * (x_nbr, y_nbr)[way] + j, way)
        return pltpu.make_async_remote_copy(
            src_ref=piece, dst_ref=piece, send_sem=diag_send.at[j, way], recv_sem=diag_recv.at[j],
            device_id=((y_nbr, x_nbr)[way], p), device_id_type=MESH,
        )

    def arrived(sem, ref):
        pltpu.make_async_copy(ref, ref, sem).wait()

    def relay(j):
        for k in range(1, 4):
            arrived(spread_recv.at[j, k - 1], stage.at[j, k - 1])
            column_all(j, k, start)

    def own(j, n):
        arrived(column_recv.at[j, z_order[n]], buf.at[2 * r + j, pl.ds(2 * z_order[n], 2)])
        plane(j, n, 0).start()
        plane(j, n, 1).start()

    def from_plane(j, n):
        for way in (n, 1 - n):
            arrived(plane_recv.at[j, way, n], half_of(2 * (x_nbr, y_nbr)[way] + j, n))
            if n == way:
                onward(j, way).start()

    def from_diag(j):
        arrived(diag_recv.at[j], buf.at[2 * diag + j])

    step = 64
    n_a = raw.shape[1]

    def split(t):
        load(t).wait()

        @pl.loop(0, n_a // step)
        def _(s):
            here = pl.ds(pl.multiple_of(s * step, step), step)
            value = raw[t, here, :]
            top = value.astype(jnp.bfloat16)
            high[t, here, :] = top
            low[t, here, :] = (value - top.astype(jnp.float32)).astype(jnp.bfloat16)

    dims = (((1,), (1,)), ((), ()))
    n_i = n_rep * rows

    def to_core(m):
        return pltpu.make_async_remote_copy(
            src_ref=part.at[m, 1 - c], dst_ref=from_core.at[m], send_sem=core_send.at[m], recv_sem=core_recv.at[m],
            device_id=(r, 2 * z + (1 - c)), device_id_type=MESH,
        )

    def multiply(t):
        g = sym[t]
        value = jnp.concatenate([buf[g, k] for k in range(n_rep)], axis=0)
        top = value.astype(jnp.bfloat16)
        rest = (value - top.astype(jnp.float32)).astype(jnp.bfloat16)
        both = lax.dot_general(
            jnp.concatenate([top, rest], axis=0), high[t], dims, preferred_element_type=jnp.float32
        )
        more = lax.dot_general(top, low[t], dims, preferred_element_type=jnp.float32)
        product = both[:n_i] + (both[n_i:] + more)
        for k in range(n_rep):
            part[t // 2, k % 2, k // 2, t % 2] = product[k * rows:(k + 1) * rows]
        if t % 2 == 1:
            to_core(t // 2).start()

    def to_z(m, k):
        there = (z + k) % 4
        return pltpu.make_async_remote_copy(
            src_ref=summed.at[m, there], dst_ref=from_z.at[m, k - 1], send_sem=z_send.at[m, k - 1],
            recv_sem=z_recv.at[m], device_id=(r, 2 * there + c), device_id_type=MESH,
        )

    def send_z(m):
        to_core(m).wait_recv()
        summed[m] = part[m, c] + from_core[m]
        for k in (2, 1, 3):
            to_z(m, k).start()

    def finish(m):
        arrived(z_recv.at[m], from_z.at[m])
        for j in range(2):
            total = (summed[m, z, j] + from_z[m, 0, j]) + (from_z[m, 1, j] + from_z[m, 2, j])
            out[sym[2 * m + j]] = 0.5 * total

    split(0)
    hear(0)
    tell(1)
    split(1)
    hear(1)
    for j in range(2):
        column_all(j, 0, start)
    split(2)
    split(3)
    split(4)
    relay(0)
    own(0,0)
    own(0,1)
    relay(1)
    own(0,2)
    own(0,3)
    own(1,0)
    own(1,1)
    own(1,2)
    own(1,3)
    multiply(0)
    from_plane(0,0)
    multiply(1)
    from_plane(0,1)
    split(5)
    send_z(0)
    multiply(2)
    from_plane(1,0)
    multiply(3)
    from_plane(1,1)
    split(6)
    split(7)
    send_z(1)
    multiply(4)
    multiply(5)
    send_z(2)
    from_diag(0)
    multiply(6)
    from_diag(1)
    multiply(7)
    finish(0)
    finish(1)
    send_z(3)
    finish(2)
    finish(3)

    for j in range(2):
        for k in range(1, 4):
            spread(j, k).wait_send()
        for k in range(4):
            column_all(j, k, wait_send)
        for way in range(2):
            for n in range(4):
                plane(j, n, way).wait_send()
            onward(j, way).wait_send()
    for m in range(4):
        to_core(m).wait_send()
        for k in range(1, 4):
            to_z(m, k).wait_send()


def per_device_kernel(amplitudes, integrals):
    n_sym, rows, _ = amplitudes.shape
    _, n_a, cols = integrals.shape
    n_rep = 8
    f32, bf16 = jnp.float32, jnp.bfloat16
    dma = pltpu.SemaphoreType.DMA
    return pl.pallas_call(
        ladder_kernel,
        out_shape=jax.ShapeDtypeStruct((n_sym, rows, n_a), f32),
        in_specs=[pl.BlockSpec(memory_space=pl.ANY)] * 2,
        out_specs=pl.BlockSpec(memory_space=pltpu.VMEM),
        scratch_shapes=[
            pltpu.VMEM((n_sym, n_a, cols), f32),
            pltpu.VMEM((n_sym, n_a, cols), bf16),
            pltpu.VMEM((n_sym, n_a, cols), bf16),
            pltpu.VMEM((2, 3, rows, amplitudes.shape[2]), f32),
            pltpu.VMEM((n_sym, n_rep, rows, cols), f32),
            pltpu.VMEM((n_sym // 2, 2, n_rep // 2, 2, rows, n_a), f32),
            pltpu.VMEM((n_sym // 2, n_rep // 2, 2, rows, n_a), f32),
            pltpu.VMEM((n_sym // 2, n_rep // 2, 2, rows, n_a), f32),
            pltpu.VMEM((n_sym // 2, n_rep // 2 - 1, 2, rows, n_a), f32),
            dma((8,)),
            dma((2, 3)),
            dma((2, 3)),
            dma((2, 4, 2)),
            dma((2, 4)),
            dma((2, 4, 2)),
            dma((2, 2, 2)),
            dma((2, 2)),
            dma((2,)),
            dma((4,)),
            dma((4,)),
            dma((4, 3)),
            dma((4,)),
            pltpu.SemaphoreType.REGULAR((2,)),
        ],
        compiler_params=pltpu.CompilerParams(
            collective_id=0, has_side_effects=True, vmem_limit_bytes=48 * 2**20
        ),
        cost_estimate=pl.CostEstimate(
            flops=6 * n_sym * n_rep * rows * n_a * cols, bytes_accessed=integrals.size * 4, transcendentals=0
        ),
    )(amplitudes, integrals)


def solution(mesh):
    in_specs = (P(None, "rep", "red"), P(None, "red", "rep"))
    out_specs = P(None, "rep", "red")
    fits = mesh.shape["red"] == 4 and mesh.shape["rep"] == 8
    return jax.shard_map(
        per_device_kernel if fits else per_device_collectives,
        mesh=mesh, in_specs=in_specs, out_specs=out_specs, check_vma=False,
    )
```

```python
import functools

import jax
import jax.numpy as jnp
from jax import lax
from jax.experimental import pallas as pl
from jax.experimental.pallas import tpu as pltpu
from jax.sharding import PartitionSpec as P

MESH = pl.DeviceIdType.MESH


def contract(rows_block, integrals):
    return jnp.einsum("gic,gac->gia", rows_block, integrals, precision=lax.Precision.HIGHEST)


def per_device_collectives(amplitudes, integrals):
    full_pairs = lax.all_gather(amplitudes, "red", axis=2, tiled=True)
    ordered = lax.all_to_all(full_pairs, "rep", split_axis=2, concat_axis=1, tiled=True)
    partial_value = contract(ordered, integrals)
    contracted = lax.psum_scatter(partial_value, "rep", scatter_dimension=1, tiled=True)
    return 0.5 * contracted


def ladder_kernel(
    amp_far, integ, out,
    amp, raw, high, low, stage, buf, part, from_core, summed, from_z,
    amp_sem, raw_sem, spread_send, spread_recv, column_send, column_recv, plane_send, plane_recv, diag_send, diag_recv,
    core_send, core_recv, z_send, z_recv, known,
):
    n_rep, rows, cols = buf.shape[1:]
    half = n_rep // 2
    r, p = lax.axis_index("red"), lax.axis_index("rep")
    z, c = p // 2, p % 2
    x, y = r % 2, r // 2
    x_nbr = (1 - x) + 2 * y
    y_nbr = x + 2 * (1 - y)
    diag = (1 - x) + 2 * (1 - y)
    order = [(r, 0), (r, 1), (x_nbr, 0), (y_nbr, 0), (x_nbr, 1), (y_nbr, 1), (diag, 0), (diag, 1)]
    sym = [2 * q + j for q, j in order]

    def load(t):
        return pltpu.make_async_copy(integ.at[sym[t]], raw.at[t], raw_sem.at[t])

    fetch = pltpu.make_async_copy(amp_far, amp, amp_sem)
    fetch.start()
    for t in range(8):
        load(t).start()

    barrier = pltpu.get_barrier_semaphore()
    last = n_rep // 2 - 1
    has_below, has_above = z > 0, z < last

    def signal(sem, red, rep):
        pl.semaphore_signal(sem, inc=1, device_id=(red, rep), device_id_type=MESH)

    for red in (diag, x_nbr, y_nbr):
        signal(barrier, red, p)
    signal(barrier, r, 2 * z + (1 - c))

    @pl.when(has_below)
    def _():
        for h in range(2):
            signal(barrier, r, 2 * (z - 1) + h)

    @pl.when(has_above)
    def _():
        for h in range(2):
            signal(barrier, r, 2 * (z + 1) + h)

    inner = jnp.logical_and(has_below, has_above)

    fetch.wait()

    @pl.when(inner)
    def _():
        pl.semaphore_wait(barrier, 8)

    @pl.when(jnp.logical_not(inner))
    def _():
        pl.semaphore_wait(barrier, 6)

    def tell(n):
        @pl.when(has_below)
        def _():
            signal(known.at[n], r, p - 2)

        @pl.when(has_above)
        def _():
            signal(known.at[n], r, p + 2)

    def hear(n):
        @pl.when(inner)
        def _():
            pl.semaphore_wait(known.at[n], 2)

        @pl.when(jnp.logical_not(inner))
        def _():
            pl.semaphore_wait(known.at[n], 1)

    near = [r, x_nbr, y_nbr, diag]

    def spread(j, k):
        return pltpu.make_async_remote_copy(
            src_ref=amp.at[2 * near[k] + j], dst_ref=stage.at[j, k - 1], send_sem=spread_send.at[j, k - 1],
            recv_sem=spread_recv.at[j, k - 1], device_id=(near[k], p), device_id_type=MESH,
        )

    def column(j, k, h, act):
        here = pl.ds(h * cols, cols)
        src = amp.at[2 * r + j, :, here] if k == 0 else stage.at[j, k - 1, :, here]
        dst = buf.at[2 * r + j, p]
        target = 2 * near[k] + h
        mine = target == p

        @pl.when(jnp.logical_not(mine))
        def _():
            act(pltpu.make_async_remote_copy(
                src_ref=src, dst_ref=dst, send_sem=column_send.at[j, k, h], recv_sem=column_recv.at[j, z],
                device_id=(r, target), device_id_type=MESH,
            ))

        if act is start:
            @pl.when(mine)
            def _():
                pltpu.make_async_copy(src, dst, column_recv.at[j, z]).start()

    def start(copy):
        copy.start()

    def wait_send(copy):
        copy.wait_send()

    def column_all(j, k, act):
        for h in range(2):
            column(j, k, h, act)

    for j in range(2):
        for k in range(1, 4):
            spread(j, k).start()
    tell(0)

    upper = z // 2
    z_order = [z, 2 * upper + 1 - z % 2, 2 - upper, 3 - 3 * upper]

    def plane(j, n, way):
        piece = buf.at[2 * r + j, pl.ds(2 * z_order[n], 2)]
        return pltpu.make_async_remote_copy(
            src_ref=piece, dst_ref=piece, send_sem=plane_send.at[j, n, way], recv_sem=plane_recv.at[j, way, n // 2],
            device_id=((x_nbr, y_nbr)[way], p), device_id_type=MESH,
        )

    def half_of(g, n):
        first = upper if n == 0 else 1 - upper
        return buf.at[g, pl.ds(first * half, half)]

    def onward(j, way):
        piece = half_of(2 * (x_nbr, y_nbr)[way] + j, way)
        return pltpu.make_async_remote_copy(
            src_ref=piece, dst_ref=piece, send_sem=diag_send.at[j, way], recv_sem=diag_recv.at[j],
            device_id=((y_nbr, x_nbr)[way], p), device_id_type=MESH,
        )

    def arrived(sem, ref):
        pltpu.make_async_copy(ref, ref, sem).wait()

    def relay(j):
        for k in range(1, 4):
            arrived(spread_recv.at[j, k - 1], stage.at[j, k - 1])
            column_all(j, k, start)

    def own(j, n):
        arrived(column_recv.at[j, z_order[n]], buf.at[2 * r + j, pl.ds(2 * z_order[n], 2)])
        plane(j, n, 0).start()
        plane(j, n, 1).start()

    def from_plane(j, n):
        for way in (n, 1 - n):
            arrived(plane_recv.at[j, way, n], half_of(2 * (x_nbr, y_nbr)[way] + j, n))
            if n == way:
                onward(j, way).start()

    def from_diag(j):
        arrived(diag_recv.at[j], buf.at[2 * diag + j])

    step = 64
    n_a = raw.shape[1]

    def split(t):
        load(t).wait()

        @pl.loop(0, n_a // step)
        def _(s):
            here = pl.ds(pl.multiple_of(s * step, step), step)
            value = raw[t, here, :]
            top = value.astype(jnp.bfloat16)
            high[t, here, :] = top
            low[t, here, :] = (value - top.astype(jnp.float32)).astype(jnp.bfloat16)

    dims = (((1,), (1,)), ((), ()))
    n_i = n_rep * rows

    def to_core(m):
        return pltpu.make_async_remote_copy(
            src_ref=part.at[m, 1 - c], dst_ref=from_core.at[m], send_sem=core_send.at[m], recv_sem=core_recv.at[m],
            device_id=(r, 2 * z + (1 - c)), device_id_type=MESH,
        )

    def multiply(t):
        g = sym[t]
        value = jnp.concatenate([buf[g, k] for k in range(n_rep)], axis=0)
        top = value.astype(jnp.bfloat16)
        rest = (value - top.astype(jnp.float32)).astype(jnp.bfloat16)
        both = lax.dot_general(
            jnp.concatenate([top, rest], axis=0), high[t], dims, preferred_element_type=jnp.float32
        )
        more = lax.dot_general(top, low[t], dims, preferred_element_type=jnp.float32)
        product = both[:n_i] + (both[n_i:] + more)
        for k in range(n_rep):
            part[t // 2, k % 2, k // 2, t % 2] = product[k * rows:(k + 1) * rows]
        if t % 2 == 1:
            to_core(t // 2).start()

    def to_z(m, k):
        there = (z + k) % 4
        return pltpu.make_async_remote_copy(
            src_ref=summed.at[m, there], dst_ref=from_z.at[m, k - 1], send_sem=z_send.at[m, k - 1],
            recv_sem=z_recv.at[m], device_id=(r, 2 * there + c), device_id_type=MESH,
        )

    def send_z(m):
        to_core(m).wait_recv()
        summed[m] = part[m, c] + from_core[m]
        for k in (2, 1, 3):
            to_z(m, k).start()

    def finish(m):
        arrived(z_recv.at[m], from_z.at[m])
        for j in range(2):
            total = (summed[m, z, j] + from_z[m, 0, j]) + (from_z[m, 1, j] + from_z[m, 2, j])
            out[sym[2 * m + j]] = 0.5 * total

    split(0)
    hear(0)
    tell(1)
    split(1)
    hear(1)
    for j in range(2):
        column_all(j, 0, start)
    split(2)
    split(3)
    split(4)
    relay(0)
    own(0,0)
    own(0,1)
    relay(1)
    own(0,2)
    own(0,3)
    own(1,0)
    own(1,1)
    own(1,2)
    own(1,3)
    multiply(0)
    from_plane(0,0)
    multiply(1)
    from_plane(0,1)
    split(5)
    send_z(0)
    multiply(2)
    from_plane(1,0)
    multiply(3)
    from_plane(1,1)
    split(6)
    split(7)
    send_z(1)
    multiply(4)
    multiply(5)
    send_z(2)
    from_diag(0)
    multiply(6)
    from_diag(1)
    multiply(7)
    finish(0)
    finish(1)
    send_z(3)
    finish(2)
    finish(3)

    for j in range(2):
        for k in range(1, 4):
            spread(j, k).wait_send()
        for k in range(4):
            column_all(j, k, wait_send)
        for way in range(2):
            for n in range(4):
                plane(j, n, way).wait_send()
            onward(j, way).wait_send()
    for m in range(4):
        to_core(m).wait_send()
        for k in range(1, 4):
            to_z(m, k).wait_send()


def per_device_kernel(amplitudes, integrals):
    n_sym, rows, _ = amplitudes.shape
    _, n_a, cols = integrals.shape
    n_rep = 8
    f32, bf16 = jnp.float32, jnp.bfloat16
    dma = pltpu.SemaphoreType.DMA
    return pl.pallas_call(
        ladder_kernel,
        out_shape=jax.ShapeDtypeStruct((n_sym, rows, n_a), f32),
        in_specs=[pl.BlockSpec(memory_space=pltpu.HBM)] * 2,
        out_specs=pl.BlockSpec(memory_space=pltpu.VMEM),
        scratch_shapes=[
            pltpu.VMEM(amplitudes.shape, f32),
            pltpu.VMEM((n_sym, n_a, cols), f32),
            pltpu.VMEM((n_sym, n_a, cols), bf16),
            pltpu.VMEM((n_sym, n_a, cols), bf16),
            pltpu.VMEM((2, 3, rows, amplitudes.shape[2]), f32),
            pltpu.VMEM((n_sym, n_rep, rows, cols), f32),
            pltpu.VMEM((n_sym // 2, 2, n_rep // 2, 2, rows, n_a), f32),
            pltpu.VMEM((n_sym // 2, n_rep // 2, 2, rows, n_a), f32),
            pltpu.VMEM((n_sym // 2, n_rep // 2, 2, rows, n_a), f32),
            pltpu.VMEM((n_sym // 2, n_rep // 2 - 1, 2, rows, n_a), f32),
            dma,
            dma((8,)),
            dma((2, 3)),
            dma((2, 3)),
            dma((2, 4, 2)),
            dma((2, 4)),
            dma((2, 4, 2)),
            dma((2, 2, 2)),
            dma((2, 2)),
            dma((2,)),
            dma((4,)),
            dma((4,)),
            dma((4, 3)),
            dma((4,)),
            pltpu.SemaphoreType.REGULAR((2,)),
        ],
        compiler_params=pltpu.CompilerParams(
            collective_id=0, has_side_effects=True, vmem_limit_bytes=48 * 2**20
        ),
        cost_estimate=pl.CostEstimate(
            flops=6 * n_sym * n_rep * rows * n_a * cols, bytes_accessed=integrals.size * 4, transcendentals=0
        ),
    )(amplitudes, integrals)


def solution(mesh):
    in_specs = (P(None, "rep", "red"), P(None, "red", "rep"))
    out_specs = P(None, "rep", "red")
    fits = mesh.shape["red"] == 4 and mesh.shape["rep"] == 8
    return jax.shard_map(
        per_device_kernel if fits else per_device_collectives,
        mesh=mesh, in_specs=in_specs, out_specs=out_specs, check_vma=False,
    )
```

```python
import functools

import jax
import jax.numpy as jnp
from jax import lax
from jax.experimental import pallas as pl
from jax.experimental.pallas import tpu as pltpu
from jax.sharding import PartitionSpec as P

MESH = pl.DeviceIdType.MESH


def contract(rows_block, integrals):
    return jnp.einsum("gic,gac->gia", rows_block, integrals, precision=lax.Precision.HIGHEST)


def per_device_collectives(amplitudes, integrals):
    full_pairs = lax.all_gather(amplitudes, "red", axis=2, tiled=True)
    ordered = lax.all_to_all(full_pairs, "rep", split_axis=2, concat_axis=1, tiled=True)
    partial_value = contract(ordered, integrals)
    contracted = lax.psum_scatter(partial_value, "rep", scatter_dimension=1, tiled=True)
    return 0.5 * contracted


def ladder_kernel(
    amp, integ, out,
    raw, high, low, stage, buf, part, from_core, summed, from_z,
    raw_sem, spread_send, spread_recv, column_send, column_recv, plane_send, plane_recv, diag_send, diag_recv,
    core_send, core_recv, z_send, z_recv, known,
):
    n_rep, rows, cols = buf.shape[1:]
    half = n_rep // 2
    r, p = lax.axis_index("red"), lax.axis_index("rep")
    z, c = p // 2, p % 2
    x, y = r % 2, r // 2
    x_nbr = (1 - x) + 2 * y
    y_nbr = x + 2 * (1 - y)
    diag = (1 - x) + 2 * (1 - y)
    order = [(r, 0), (r, 1), (x_nbr, 0), (y_nbr, 0), (x_nbr, 1), (y_nbr, 1), (diag, 0), (diag, 1)]
    sym = [2 * q + j for q, j in order]

    def load(t):
        return pltpu.make_async_copy(integ.at[sym[t]], raw.at[t], raw_sem.at[t])

    for t in range(8):
        load(t).start()

    barrier = pltpu.get_barrier_semaphore()
    last = n_rep // 2 - 1
    has_below, has_above = z > 0, z < last

    def signal(sem, red, rep):
        pl.semaphore_signal(sem, inc=1, device_id=(red, rep), device_id_type=MESH)

    for red in (diag, x_nbr, y_nbr):
        signal(barrier, red, p)
    signal(barrier, r, 2 * z + (1 - c))

    @pl.when(has_below)
    def _():
        for h in range(2):
            signal(barrier, r, 2 * (z - 1) + h)

    @pl.when(has_above)
    def _():
        for h in range(2):
            signal(barrier, r, 2 * (z + 1) + h)

    inner = jnp.logical_and(has_below, has_above)


    @pl.when(inner)
    def _():
        pl.semaphore_wait(barrier, 8)

    @pl.when(jnp.logical_not(inner))
    def _():
        pl.semaphore_wait(barrier, 6)

    def tell(n):
        @pl.when(has_below)
        def _():
            signal(known.at[n], r, p - 2)

        @pl.when(has_above)
        def _():
            signal(known.at[n], r, p + 2)

    def hear(n):
        @pl.when(inner)
        def _():
            pl.semaphore_wait(known.at[n], 2)

        @pl.when(jnp.logical_not(inner))
        def _():
            pl.semaphore_wait(known.at[n], 1)

    near = [r, x_nbr, y_nbr, diag]

    def spread(j, k):
        return pltpu.make_async_remote_copy(
            src_ref=amp.at[2 * near[k] + j], dst_ref=stage.at[j, k - 1], send_sem=spread_send.at[j, k - 1],
            recv_sem=spread_recv.at[j, k - 1], device_id=(near[k], p), device_id_type=MESH,
        )

    def column(j, k, h, act):
        here = pl.ds(h * cols, cols)
        src = amp.at[2 * r + j, :, here] if k == 0 else stage.at[j, k - 1, :, here]
        dst = buf.at[2 * r + j, p]
        target = 2 * near[k] + h
        mine = target == p

        @pl.when(jnp.logical_not(mine))
        def _():
            act(pltpu.make_async_remote_copy(
                src_ref=src, dst_ref=dst, send_sem=column_send.at[j, k, h], recv_sem=column_recv.at[j, z],
                device_id=(r, target), device_id_type=MESH,
            ))

        if act is start:
            @pl.when(mine)
            def _():
                pltpu.make_async_copy(src, dst, column_recv.at[j, z]).start()

    def start(copy):
        copy.start()

    def wait_send(copy):
        copy.wait_send()

    def column_all(j, k, act):
        for h in range(2):
            column(j, k, h, act)

    for j in range(2):
        for k in range(1, 4):
            spread(j, k).start()
    tell(0)

    upper = z // 2
    z_order = [z, 2 * upper + 1 - z % 2, 2 - upper, 3 - 3 * upper]

    def plane(j, n, way):
        piece = buf.at[2 * r + j, pl.ds(2 * z_order[n], 2)]
        return pltpu.make_async_remote_copy(
            src_ref=piece, dst_ref=piece, send_sem=plane_send.at[j, n, way], recv_sem=plane_recv.at[j, way, n // 2],
            device_id=((x_nbr, y_nbr)[way], p), device_id_type=MESH,
        )

    def half_of(g, n):
        first = upper if n == 0 else 1 - upper
        return buf.at[g, pl.ds(first * half, half)]

    def onward(j, way):
        piece = half_of(2 * (x_nbr, y_nbr)[way] + j, way)
        return pltpu.make_async_remote_copy(
            src_ref=piece, dst_ref=piece, send_sem=diag_send.at[j, way], recv_sem=diag_recv.at[j],
            device_id=((y_nbr, x_nbr)[way], p), device_id_type=MESH,
        )

    def arrived(sem, ref):
        pltpu.make_async_copy(ref, ref, sem).wait()

    def relay(j):
        for k in range(1, 4):
            arrived(spread_recv.at[j, k - 1], stage.at[j, k - 1])
            column_all(j, k, start)

    def own(j, n):
        arrived(column_recv.at[j, z_order[n]], buf.at[2 * r + j, pl.ds(2 * z_order[n], 2)])
        plane(j, n, 0).start()
        plane(j, n, 1).start()

    def from_plane(j, n):
        for way in (n, 1 - n):
            arrived(plane_recv.at[j, way, n], half_of(2 * (x_nbr, y_nbr)[way] + j, n))
            if n == way:
                onward(j, way).start()

    def from_diag(j):
        arrived(diag_recv.at[j], buf.at[2 * diag + j])

    step = 64
    n_a = raw.shape[1]

    def split(t):
        load(t).wait()

        @pl.loop(0, n_a // step)
        def _(s):
            here = pl.ds(pl.multiple_of(s * step, step), step)
            value = raw[t, here, :]
            top = value.astype(jnp.bfloat16)
            high[t, here, :] = top
            low[t, here, :] = (value - top.astype(jnp.float32)).astype(jnp.bfloat16)

    dims = (((1,), (1,)), ((), ()))
    n_i = n_rep * rows

    def to_core(m):
        return pltpu.make_async_remote_copy(
            src_ref=part.at[m, 1 - c], dst_ref=from_core.at[m], send_sem=core_send.at[m], recv_sem=core_recv.at[m],
            device_id=(r, 2 * z + (1 - c)), device_id_type=MESH,
        )

    def multiply(t):
        g = sym[t]
        value = jnp.concatenate([buf[g, k] for k in range(n_rep)], axis=0)
        top = value.astype(jnp.bfloat16)
        rest = (value - top.astype(jnp.float32)).astype(jnp.bfloat16)
        both = lax.dot_general(
            jnp.concatenate([top, rest], axis=0), high[t], dims, preferred_element_type=jnp.float32
        )
        more = lax.dot_general(top, low[t], dims, preferred_element_type=jnp.float32)
        product = both[:n_i] + (both[n_i:] + more)
        for k in range(n_rep):
            part[t // 2, k % 2, k // 2, t % 2] = product[k * rows:(k + 1) * rows]
        if t % 2 == 1:
            to_core(t // 2).start()

    def to_z(m, k):
        there = (z + k) % 4
        return pltpu.make_async_remote_copy(
            src_ref=summed.at[m, there], dst_ref=from_z.at[m, k - 1], send_sem=z_send.at[m, k - 1],
            recv_sem=z_recv.at[m], device_id=(r, 2 * there + c), device_id_type=MESH,
        )

    def send_z(m):
        to_core(m).wait_recv()
        summed[m] = part[m, c] + from_core[m]
        for k in (2, 1, 3):
            to_z(m, k).start()

    def finish(m):
        arrived(z_recv.at[m], from_z.at[m])
        for j in range(2):
            total = (summed[m, z, j] + from_z[m, 0, j]) + (from_z[m, 1, j] + from_z[m, 2, j])
            out[sym[2 * m + j]] = 0.5 * total

    split(0)
    hear(0)
    tell(1)
    split(1)
    hear(1)
    for j in range(2):
        column_all(j, 0, start)
    split(2)
    split(3)
    split(4)
    relay(0)
    split(5)
    own(0,0)
    own(0,1)
    relay(1)
    split(6)
    own(0,2)
    own(0,3)
    own(1,0)
    own(1,1)
    own(1,2)
    own(1,3)
    multiply(0)
    split(7)
    from_plane(0,0)
    multiply(1)
    from_plane(0,1)
    send_z(0)
    multiply(2)
    from_plane(1,0)
    multiply(3)
    from_plane(1,1)
    send_z(1)
    multiply(4)
    multiply(5)
    send_z(2)
    from_diag(0)
    multiply(6)
    from_diag(1)
    multiply(7)
    finish(0)
    finish(1)
    send_z(3)
    finish(2)
    finish(3)

    for j in range(2):
        for k in range(1, 4):
            spread(j, k).wait_send()
        for k in range(4):
            column_all(j, k, wait_send)
        for way in range(2):
            for n in range(4):
                plane(j, n, way).wait_send()
            onward(j, way).wait_send()
    for m in range(4):
        to_core(m).wait_send()
        for k in range(1, 4):
            to_z(m, k).wait_send()


def per_device_kernel(amplitudes, integrals):
    n_sym, rows, _ = amplitudes.shape
    _, n_a, cols = integrals.shape
    n_rep = 8
    f32, bf16 = jnp.float32, jnp.bfloat16
    dma = pltpu.SemaphoreType.DMA
    return pl.pallas_call(
        ladder_kernel,
        out_shape=jax.ShapeDtypeStruct((n_sym, rows, n_a), f32),
        in_specs=[pl.BlockSpec(memory_space=pl.ANY)] * 2,
        out_specs=pl.BlockSpec(memory_space=pltpu.VMEM),
        scratch_shapes=[
            pltpu.VMEM((n_sym, n_a, cols), f32),
            pltpu.VMEM((n_sym, n_a, cols), bf16),
            pltpu.VMEM((n_sym, n_a, cols), bf16),
            pltpu.VMEM((2, 3, rows, amplitudes.shape[2]), f32),
            pltpu.VMEM((n_sym, n_rep, rows, cols), f32),
            pltpu.VMEM((n_sym // 2, 2, n_rep // 2, 2, rows, n_a), f32),
            pltpu.VMEM((n_sym // 2, n_rep // 2, 2, rows, n_a), f32),
            pltpu.VMEM((n_sym // 2, n_rep // 2, 2, rows, n_a), f32),
            pltpu.VMEM((n_sym // 2, n_rep // 2 - 1, 2, rows, n_a), f32),
            dma((8,)),
            dma((2, 3)),
            dma((2, 3)),
            dma((2, 4, 2)),
            dma((2, 4)),
            dma((2, 4, 2)),
            dma((2, 2, 2)),
            dma((2, 2)),
            dma((2,)),
            dma((4,)),
            dma((4,)),
            dma((4, 3)),
            dma((4,)),
            pltpu.SemaphoreType.REGULAR((2,)),
        ],
        compiler_params=pltpu.CompilerParams(
            collective_id=0, has_side_effects=True, vmem_limit_bytes=48 * 2**20
        ),
        cost_estimate=pl.CostEstimate(
            flops=6 * n_sym * n_rep * rows * n_a * cols, bytes_accessed=integrals.size * 4, transcendentals=0
        ),
    )(amplitudes, integrals)


def solution(mesh):
    in_specs = (P(None, "rep", "red"), P(None, "red", "rep"))
    out_specs = P(None, "rep", "red")
    fits = mesh.shape["red"] == 4 and mesh.shape["rep"] == 8
    return jax.shard_map(
        per_device_kernel if fits else per_device_collectives,
        mesh=mesh, in_specs=in_specs, out_specs=out_specs, check_vma=False,
    )
```
